256 devices in a mesh: section: 2 (over core), expert: 16 (over y, x), dp: 8 (over z).
Axes of the slice: x: 4, y: 4, z: 8, core: 2. Of those that a mesh axis runs over, the one named last changes fastest.
Arguments:
- tokens: bfloat16 [2, 8192, 768], P('section', 'dp', 'expert'), may hold values from -6 to 6
- norm_gain: bfloat16 [2, 768], P('section', 'expert'), may hold values from 0.099609375 to 1.8984375
- w_gate: bfloat16 [2, 768, 12288], P('section', None, 'expert'), may hold values from -0.21875 to 0.21875
- w_up: bfloat16 [2, 768, 12288], P('section', None, 'expert'), may hold values from -0.21875 to 0.21875
- w_down: bfloat16 [2, 12288, 768], P('section', 'expert'), may hold values from -0.75 to 0.75
- expert_ids: int32 [2, 4, 8192, 2], P('section', None, 'dp'), may hold values from 0 to 7, all different within a row; in each aligned block of 1024 rows (0 to 1023, 1024 to 2047, ..., all dimensions but the last counted through in order) at most 512 rows name the same one
- gate_logits: float32 [2, 4, 8192, 2], P('section', None, 'dp'), may hold values from -0.3 to 0.3
Outputs:
- carried: bfloat16 [2, 8192, 768], P('section', 'dp', 'expert')
The draws below stay inside these ranges and needn't reach their ends.
Inputs may be any that keep to these rules, and one draw needn't show every extreme that they name: `expert_ids`: A row names two different experts. In each block of 1024 rows that one index of dp holds for one section and stop, no expert is named by more than 512 rows, and one is named by exactly 512.
All inputs are finite; a program needn't handle non-finite values.
Results may differ from the reference program's by a relative error of at most 0.019.
Values may be sent and summed in bfloat16 or wider, within the bound.
A program may use at most 64 MiB of HBM per device.

```python
import math
import jax
import jax.numpy as jnp
import numpy as np
from jax import lax

D = 768
FFW = 768
STOPS = 4
ROWS_DEV = 1024
EXPERTS = 8
FFN = 1536
FF_ALL = 12288
CAPACITY = 512
ROWS = 8192
MICRO = 2
N_SECTION = 2


def draw_w_down(key, part):
    key = jax.random.fold_in(key, 7)
    shared_key, jitter_key = jax.random.split(key)
    shared = 1.2 * jnp.clip(jax.random.normal(shared_key, (N_SECTION, 1, D), jnp.float32), -3.0, 3.0)
    jitter = 0.7 * jnp.clip(jax.random.normal(jitter_key, (N_SECTION, FF_ALL, D), jnp.float32), -3.0, 3.0)
    return ((shared + jitter) * FFN ** (-0.5)).astype(jnp.bfloat16)


def levels(key, dims, cuts, low, top_value):
    gain, own = 1.0, jax.random.fold_in(key, 6)
    for dim, blocks in cuts:
        steps = jnp.exp(jax.random.uniform(jax.random.fold_in(own, dim), (blocks,), jnp.float32, low / len(cuts), top_value / len(cuts)))
        gain = gain * jnp.repeat(steps, dims[dim] // blocks).reshape([-1 if axis == dim else 1 for axis in range(len(dims))])
    return gain


def shared_out(rng, own, number, rows, amount, top, bound, slope):
    sequence = jax.random.permutation(rng, amount)
    heavy_load, ordinary = portions_of(amount, rows * top, bound, slope, True), portions_of(amount, rows * top, bound, slope, False)
    places = jnp.arange(amount)

    def named(lengths, offset_by):
        used = int((lengths > 0).sum())
        fixed = max(1, used // 4)
        shifted = fixed + (places - fixed + offset_by * (used - fixed)) % max(1, amount - fixed)
        return jnp.zeros((amount,), jnp.int32).at[sequence[jnp.where(places < fixed, places, shifted)]].set(jnp.asarray(lengths, jnp.int32))

    lengths = jnp.where(number % 4 == 0, named(heavy_load, number // 4), named(ordinary, number - number // 4 - 1))
    mixed = jax.random.permutation(jax.random.fold_in(own, 3), amount)
    donor, receiver = mixed[0:amount // 2 * 2:2], mixed[1:amount // 2 * 2:2]
    room = jnp.minimum(lengths[donor] - 1, bound - lengths[receiver]) // 2
    room = jnp.where((donor == sequence[0]) | (receiver == sequence[0]) | (lengths[receiver] == 0), 0, jnp.maximum(room, 0))
    shifted = jax.random.randint(jax.random.fold_in(own, 4), (amount // 2,), 0, 1 << 20) % (room + 1)
    lengths = lengths.at[donor].add(-shifted).at[receiver].add(shifted)
    items = jnp.searchsorted(jnp.cumsum(lengths), jnp.arange(rows * top), side="right").astype(jnp.int32)
    table = items.reshape(top, rows).T
    table = table[jax.random.permutation(jax.random.fold_in(own, 1), rows)]
    offset_by = jax.random.randint(jax.random.fold_in(own, 2), (rows, 1), 0, top)
    return jnp.take_along_axis(table, (jnp.arange(top)[None, :] + offset_by) % top, axis=1)


def portions_of(amount, total, bound, lean, full):
    portions = [(1 << 20) // math.isqrt(standing ** lean) + 1 for standing in range(1, amount + 1)]
    largest = bound if full else min(bound, max(-(-total // amount), total * portions[0] // sum(portions)))
    least = 1 if total - largest >= amount - 1 else 0
    counts, surplus = [largest] + [least] * (amount - 1), total - largest - least * (amount - 1)
    while surplus > 0:
        candidates = [i for i in range(1, amount) if counts[i] < largest] or [i for i in range(1, amount) if counts[i] < bound]
        pool, budget = sum([portions[i] for i in candidates]), surplus
        for i in candidates:
            addition = min(bound - counts[i], max(1, budget * portions[i] // pool), surplus)
            counts[i] = counts[i] + addition
            surplus = surplus - addition
    return np.array(counts)


def normal_values(key, extent, deviation, most, pieces=(), kind=jnp.bfloat16):
    entries = deviation * jax.random.normal(key, extent, jnp.float32)
    if pieces:
        entries = entries * levels(key, extent, pieces, -0.22, 0.18)
    return jnp.clip(entries, -most, most).astype(kind)


def setup_inputs(seed: int = 0) -> dict:
    seeds = jax.random.split(jax.random.key(seed), 8)
    tokens = normal_values(seeds[0], (MICRO, ROWS, D), 1.0, 6.0, ((0, 2), (1, 8), (2, 16)))
    norm_gain = jnp.clip(1.0 + 0.18 * jax.random.normal(seeds[1], (N_SECTION, D), jnp.float32), 0.099609375, 1.8984375).astype(jnp.bfloat16)
    w_gate = normal_values(seeds[2], (N_SECTION, D, FF_ALL), D ** -0.5, 0.21875, ((0, 2), (2, 16)))
    w_up = normal_values(seeds[3], (N_SECTION, D, FF_ALL), D ** -0.5, 0.21875, ((0, 2), (2, 16)))
    w_down = draw_w_down(jax.random.fold_in(seeds[7], 71), 0)
    expert_ids_keys = jax.random.split(jax.random.fold_in(seeds[5], 1), N_SECTION * STOPS * ROWS // ROWS_DEV)
    expert_ids_turns = jax.random.permutation(jax.random.fold_in(seeds[5], 3), N_SECTION * STOPS * ROWS // ROWS_DEV)
    expert_ids = jax.vmap(lambda own, number: shared_out(jax.random.fold_in(seeds[5], 2), own, number, ROWS_DEV, EXPERTS, 2, CAPACITY, 2))(expert_ids_keys, expert_ids_turns).reshape((N_SECTION, STOPS, ROWS, 2))
    gate_logits = jnp.clip(jax.random.uniform(seeds[6], (N_SECTION, STOPS, ROWS, 2), jnp.float32, -0.3, 0.3) * levels(seeds[6], (N_SECTION, STOPS, ROWS, 2), ((0, 2), (2, 8)), -0.4, 0.0), -0.3, 0.3)
    return {"tokens": tokens, "norm_gain": norm_gain, "w_gate": w_gate, "w_up": w_up, "w_down": w_down, "expert_ids": expert_ids, "gate_logits": gate_logits}


def half_output(normed, gate_w, up_w, down_w):
    gate_val = jnp.dot(normed, gate_w, preferred_element_type=jnp.float32)
    up_val = jnp.dot(normed, up_w, preferred_element_type=jnp.float32)
    hidden = (jax.nn.silu(gate_val) * up_val).astype(jnp.bfloat16)
    return jnp.dot(hidden, down_w, preferred_element_type=jnp.float32).astype(jnp.bfloat16)

def apply_layer(acts, gain_row, gate_w, up_w, down_w, route_ids, logits):
    widened = acts.astype(jnp.float32)
    mean_sq = lax.optimization_barrier(jnp.mean(widened * widened, axis=1, keepdims=True))
    normed = (widened * lax.rsqrt(mean_sq + 1e-05) * gain_row.astype(jnp.float32)).astype(jnp.bfloat16)
    gate_sets = gate_w.reshape(D, EXPERTS, 2, FFW).transpose(1, 2, 0, 3)
    up_sets = up_w.reshape(D, EXPERTS, 2, FFW).transpose(1, 2, 0, 3)
    down_sets = down_w.reshape(EXPERTS, 2, FFW, D)

    def per_expert(weights):
        first_half = half_output(normed, weights[0][0], weights[1][0], weights[2][0]).astype(jnp.float32)
        second_half = half_output(normed, weights[0][1], weights[1][1], weights[2][1]).astype(jnp.float32)
        return first_half + second_half
    expert_outs = lax.map(per_expert, (gate_sets, up_sets, down_sets))
    row_index = jnp.arange(acts.shape[0], dtype=jnp.int32)
    first_pick = expert_outs[route_ids[:, 0], row_index]
    second_pick = expert_outs[route_ids[:, 1], row_index]
    weight_one = jax.nn.sigmoid(logits[:, 0] - logits[:, 1])
    weight_two = jax.nn.sigmoid(logits[:, 1] - logits[:, 0])
    updated = widened + weight_one[:, None] * first_pick + weight_two[:, None] * second_pick
    return updated.astype(jnp.bfloat16)

def reference(tokens, norm_gain, w_gate, w_up, w_down, expert_ids, gate_logits):
    carried = tokens
    for stop_num in range(STOPS):
        carried = jnp.stack([apply_layer(carried[section_num], norm_gain[section_num], w_gate[section_num], w_up[section_num], w_down[section_num], expert_ids[section_num, stop_num], gate_logits[section_num, stop_num]) for section_num in range(N_SECTION)])
        carried = jnp.roll(carried, 1, axis=0)
    return carried
```

```python
import functools

import jax
import jax.numpy as jnp
from jax import lax
from jax.experimental import pallas as pl
from jax.experimental.pallas import tpu as pltpu
from jax.sharding import PartitionSpec as P

D = 768
STOPS = 4
GROUPS = 4
SIDE = 4
SLICE = 48
MESH = pl.DeviceIdType.MESH


def kernel(
    lanes,
    tokens_ref, gain_ref, weight_ref, gate_ref, up_ref, down_ref,
    out_ref,
    gathered, partial, returned, summed, last, held, final, gain_all,
    gate_t, up_t, down_t, raw,
    recv_sem, send_sem, final_recv, final_send, gain_recv, gain_send, load_sem,
):
    section = lax.axis_index("section")
    chip = lax.axis_index("expert")
    plane = lax.axis_index("dp")
    y, x = chip // SIDE, lax.rem(chip, SIDE)

    def device(core, row, column):
        return (core, row * SIDE + column, plane)

    other = 1 - section
    y_peers = [lax.rem(y + step, SIDE) for step in range(1, SIDE)]
    x_peers = [lax.rem(x + step, SIDE) for step in range(1, SIDE)]

    loads = [
        pltpu.make_async_copy(source, raw.at[i], load_sem.at[i])
        for i, source in enumerate((gate_ref, up_ref, down_ref))
    ]
    for load in loads:
        load.start()

    barrier = pltpu.get_barrier_semaphore()
    partners = [device(other, y, x)]
    for core in (section, other):
        partners += [device(core, row, x) for row in y_peers]
        partners += [device(core, y, column) for column in x_peers]
    for partner in partners:
        pl.semaphore_signal(barrier, inc=1, device_id=partner, device_id_type=MESH)
    pl.semaphore_wait(barrier, len(partners))

    def send(source, target, send_at, recv_at, to):
        pltpu.make_async_remote_copy(
            src_ref=source, dst_ref=target, send_sem=send_at, recv_sem=recv_at,
            device_id=to, device_id_type=MESH,
        ).start()

    def wait_blocks(sem, rows, blocks):
        room = gathered.at[0, 0, 0] if rows == 16 else None
        del room
        view = returned.at[0, 0].reshape(2 * SIDE * SIDE, SLICE, lanes).at[pl.ds(0, blocks)]
        pltpu.make_async_copy(view, view, sem).wait()

    for group in range(GROUPS):
        to_recv, to_send = recv_sem.at[0, 0, group], send_sem.at[0, 0, group]
        for half in range(2):
            block = tokens_ref.at[group, half]
            mine = gathered.at[0, group, half, y, x]
            pltpu.make_async_copy(block, mine, to_recv).start()
            for peer in y_peers if half == 0 else x_peers:
                to = device(section, peer, x) if half == 0 else device(section, y, peer)
                send(block, mine, to_send, to_recv, to)
    pltpu.make_async_copy(gain_ref, gain_all.at[y, x], gain_recv.at[0]).start()
    for peer in y_peers:
        send(gain_ref, gain_all.at[y, x], gain_send.at[0], gain_recv.at[0], device(section, peer, x))

    for i, target in enumerate((gate_t, up_t, down_t)):
        loads[i].wait()
        target[...] = raw[i].T

    def wait_gain(sem, blocks):
        view = gain_all.reshape(SIDE * SIDE, SLICE, 128).at[pl.ds(0, blocks)]
        pltpu.make_async_copy(view, view, sem).wait()

    wait_gain(gain_recv.at[0], 4)
    for peer in x_peers:
        send(gain_all.at[:, x], gain_all.at[:, x], gain_send.at[1], gain_recv.at[1], device(section, y, peer))

    def spread(t, g):
        wait_blocks(recv_sem.at[0, t, g], 0, 8)
        to_recv, to_send = recv_sem.at[1, t, g], send_sem.at[1, t, g]
        for i in range(3):
            column = gathered.at[t, g, 0, :, x]
            send(column, column, to_send, to_recv, device(section, y, x_peers[i]))
            row = gathered.at[t, g, 1, y]
            send(row, row, to_send, to_recv, device(section, y_peers[i], x))

    def compute(t, g):
        wait_blocks(recv_sem.at[1, t, g], 0, 24)

        @pl.when((t == 0) & (g == 0))
        def _():
            wait_gain(gain_recv.at[1], 12)

        acts = jnp.concatenate(
            [gathered[t, g, half].reshape(D, lanes) for half in range(2)], axis=1
        ).astype(jnp.float32)
        inverse = lax.rsqrt(jnp.sum(acts * acts, axis=0, keepdims=True) / D + 1e-05)
        gain = gain_all[...].reshape(D, 128).astype(jnp.float32)
        gain = jnp.concatenate([gain] * (2 * lanes // 128), axis=1)
        normed = (acts * inverse * gain).astype(jnp.bfloat16)
        gate_val = jnp.dot(gate_t[...], normed, preferred_element_type=jnp.float32)
        up_val = jnp.dot(up_t[...], normed, preferred_element_type=jnp.float32)
        hidden = (jax.nn.silu(gate_val) * up_val).astype(jnp.bfloat16)
        outcome = jnp.dot(down_t[...], hidden, preferred_element_type=jnp.float32)
        outcome = (outcome * weight_ref[t, g]).astype(jnp.bfloat16)
        for half in range(2):
            partial[t, g, half] = outcome[:, half * lanes:(half + 1) * lanes].reshape(SIDE, SIDE, SLICE, lanes)
        to_recv, to_send = recv_sem.at[2, t, g], send_sem.at[2, t, g]
        for i in range(3):
            send(partial.at[t, g, 0, :, x_peers[i]], returned.at[t, g, 0, x], to_send, to_recv,
                 device(section, y, x_peers[i]))
            send(partial.at[t, g, 1, y_peers[i]], returned.at[t, g, 1, y], to_send, to_recv,
                 device(section, y_peers[i], x))

    def collect(t, g):
        wait_blocks(recv_sem.at[2, t, g], 0, 24)
        total = partial[t, g, 0, :, x].astype(jnp.float32)
        for peer in x_peers:
            total = total + returned[t, g, 0, peer].astype(jnp.float32)
        summed[t, g, 0] = total.astype(jnp.bfloat16)
        total = partial[t, g, 1, y].astype(jnp.float32)
        for peer in y_peers:
            total = total + returned[t, g, 1, peer].astype(jnp.float32)
        summed[t, g, 1] = total.astype(jnp.bfloat16)
        to_recv, to_send = recv_sem.at[3, t, g], send_sem.at[3, t, g]
        for i in range(3):
            send(summed.at[t, g, 0, y_peers[i]], last.at[t, g, 0, y], to_send, to_recv,
                 device(section, y_peers[i], x))
            send(summed.at[t, g, 1, x_peers[i]], last.at[t, g, 1, x], to_send, to_recv,
                 device(section, y, x_peers[i]))

    def finish(t, g):
        wait_blocks(recv_sem.at[3, t, g], 0, 6)
        for half in range(2):
            own, peers = (y, y_peers) if half == 0 else (x, x_peers)
            total = summed[t, g, half, own].astype(jnp.float32)
            for peer in peers:
                total = total + last[t, g, half, peer].astype(jnp.float32)
            total = gathered[t, g, half, y, x].astype(jnp.float32) + total
            held[t, g, half] = total.astype(jnp.bfloat16)

        @pl.when(t < STOPS - 1)
        def _():
            later = jnp.minimum(t + 1, STOPS - 1)
            to_recv, to_send = recv_sem.at[0, later, g], send_sem.at[0, later, g]
            for half in range(2):
                target = gathered.at[later, g, half, y, x]
                send(held.at[t, g, half], target, to_send, to_recv, device(other, y, x))
                for peer in y_peers if half == 0 else x_peers:
                    to = device(other, peer, x) if half == 0 else device(other, y, peer)
                    send(held.at[t, g, half], target, to_send, to_recv, to)

        @pl.when(t == STOPS - 1)
        def _():
            send(held.at[t, g], final.at[g], final_send.at[g], final_recv.at[g], device(other, y, x))

    stages = (spread, compute, collect, finish)
    count = len(stages)

    def tick(now, carry):
        for k, stage in enumerate(stages):
            g = lax.rem(now - k + count, count)
            n = now - g

            @pl.when((n >= 0) & (n < count * STOPS))
            def _(stage=stage, g=g, n=n):
                stage(jnp.maximum(n, 0) // count, g)
        return carry

    lax.fori_loop(0, count * STOPS + GROUPS - 1, tick, 0)

    for g in range(GROUPS):
        wait_blocks(final_recv.at[g], 0, 2)
        wait_blocks(final_send.at[g], 0, 2)
        out_ref[g] = final[g]
    wait_gain(gain_send.at[0], 3)
    wait_gain(gain_send.at[1], 12)

    def settle(t, carry):
        for g in range(GROUPS):
            for k, blocks in enumerate((8, 24, 24, 6)):
                if k:
                    wait_blocks(send_sem.at[k, t, g], 0, blocks)

            @pl.when(t == 0)
            def _():
                wait_blocks(send_sem.at[0, 0, g], 0, 6)

            @pl.when(t > 0)
            def _():
                wait_blocks(send_sem.at[0, t, g], 0, 8)
        return carry

    lax.fori_loop(0, STOPS, settle, 0)


def per_device(tokens, norm_gain, w_gate, w_up, w_down, expert_ids, gate_logits):
    rows, width = tokens.shape[1:]
    lanes = rows // (2 * GROUPS)
    split = tokens[0].reshape(GROUPS, 2, lanes, width).transpose(0, 1, 3, 2)
    gain = jnp.broadcast_to(norm_gain[0][:, None], (width, 128))
    expert = lax.axis_index("expert") // 2
    ids, logits = expert_ids[0], gate_logits[0]
    weight_one = jax.nn.sigmoid(logits[..., 0] - logits[..., 1])
    weight_two = jax.nn.sigmoid(logits[..., 1] - logits[..., 0])
    weight = jnp.where(ids[..., 0] == expert, weight_one, 0.0) + jnp.where(ids[..., 1] == expert, weight_two, 0.0)
    weight = weight.reshape(STOPS, GROUPS, 1, 2 * lanes)
    block = (STOPS, GROUPS, 2)
    vmem = pl.BlockSpec(memory_space=pltpu.VMEM)
    out = pl.pallas_call(
        functools.partial(kernel, lanes),
        out_shape=jax.ShapeDtypeStruct((GROUPS, 2, width, lanes), jnp.bfloat16),
        in_specs=[vmem] * 3 + [pl.BlockSpec(memory_space=pl.ANY)] * 3,
        out_specs=vmem,
        scratch_shapes=[
            pltpu.VMEM(block + (SIDE, SIDE, width, lanes), jnp.bfloat16),
            pltpu.VMEM(block + (SIDE, SIDE, width, lanes), jnp.bfloat16),
            pltpu.VMEM(block + (SIDE, SIDE, width, lanes), jnp.bfloat16),
            pltpu.VMEM(block + (SIDE, width, lanes), jnp.bfloat16),
            pltpu.VMEM(block + (SIDE, width, lanes), jnp.bfloat16),
            pltpu.VMEM(block + (width, lanes), jnp.bfloat16),
            pltpu.VMEM((GROUPS, 2, width, lanes), jnp.bfloat16),
            pltpu.VMEM((SIDE, SIDE, width, 128), jnp.bfloat16),
            pltpu.VMEM((D, D), jnp.bfloat16),
            pltpu.VMEM((D, D), jnp.bfloat16),
            pltpu.VMEM((D, D), jnp.bfloat16),
            pltpu.VMEM((3, D, D), jnp.bfloat16),
            pltpu.SemaphoreType.DMA((4, STOPS, GROUPS)),
            pltpu.SemaphoreType.DMA((4, STOPS, GROUPS)),
            pltpu.SemaphoreType.DMA((GROUPS,)),
            pltpu.SemaphoreType.DMA((GROUPS,)),
            pltpu.SemaphoreType.DMA((2,)),
            pltpu.SemaphoreType.DMA((2,)),
            pltpu.SemaphoreType.DMA((3,)),
        ],
        compiler_params=pltpu.CompilerParams(
            collective_id=0, has_side_effects=True, vmem_limit_bytes=56 << 20
        ),
    )(split, gain, weight, w_gate[0], w_up[0], w_down[0])
    return out.transpose(0, 1, 3, 2).reshape(1, rows, width)


def solution(mesh):
    placed = (
        P("section", "dp", "expert"),
        P("section", "expert"),
        P("section", None, "expert"),
        P("section", None, "expert"),
        P("section", "expert", None),
        P("section", None, "dp", None),
        P("section", None, "dp", None),
    )
    return jax.shard_map(
        per_device,
        mesh=mesh,
        in_specs=placed,
        out_specs=P("section", "dp", "expert"),
        check_vma=False,
    )
```

```python
import jax
import jax.numpy as jnp
from jax import lax
from jax.experimental import pallas as pl
from jax.experimental.pallas import tpu as pltpu
from jax.sharding import PartitionSpec as P

D = 768
STOPS = 4
GROUPS = 4
SIDE = 4
SLICE = 48
PIECE = 256
MESH = pl.DeviceIdType.MESH


def kernel(
    tokens_ref, gain_ref, ids_ref, logits_ref, gate_ref, up_ref, down_ref,
    out_ref,
    gathered, partial, returned, summed, last, held, final, gain_own, gain_all, weight,
    gate_t, up_t, down_t, raw,
    recv_sem, send_sem, final_recv, final_send, gain_recv, gain_send, load_sem,
):
    section = lax.axis_index("section")
    chip = lax.axis_index("expert")
    plane = lax.axis_index("dp")
    y, x = chip // SIDE, lax.rem(chip, SIDE)
    lanes = gathered.shape[-1]

    def device(core, row, column):
        return (core, row * SIDE + column, plane)

    other = 1 - section
    y_peers = [lax.rem(y + step, SIDE) for step in range(1, SIDE)]
    x_peers = [lax.rem(x + step, SIDE) for step in range(1, SIDE)]

    barrier = pltpu.get_barrier_semaphore()
    partners = [device(other, y, x)]
    for core in (section, other):
        partners += [device(core, row, x) for row in y_peers]
        partners += [device(core, y, column) for column in x_peers]
    for partner in partners:
        pl.semaphore_signal(barrier, inc=1, device_id=partner, device_id_type=MESH)
    loads = [
        pltpu.make_async_copy(source, raw.at[i], load_sem.at[i])
        for i, source in enumerate((gate_ref, up_ref, down_ref))
    ]
    for load in loads:
        load.start()
    gain_row = jnp.broadcast_to(gain_ref[...].astype(jnp.float32), (128, SLICE))
    gain_own[...] = gain_row.T.astype(jnp.bfloat16)
    pl.semaphore_wait(barrier, len(partners))

    def send(source, target, send_at, recv_at, to):
        pltpu.make_async_remote_copy(
            src_ref=source, dst_ref=target, send_sem=send_at, recv_sem=recv_at,
            device_id=to, device_id_type=MESH,
        ).start()

    def wait_blocks(sem, blocks):
        view = gathered.at[0, 0].reshape(2 * SIDE * SIDE, SLICE, lanes).at[pl.ds(0, blocks)]
        pltpu.make_async_copy(view, view, sem).wait()

    def wait_gain(sem, blocks):
        view = gain_all.reshape(SIDE * SIDE, SLICE, 128).at[pl.ds(0, blocks)]
        pltpu.make_async_copy(view, view, sem).wait()

    def chip_at(half, on_line, across):
        return (across, on_line) if half == 0 else (on_line, across)

    mine = [(x, y), (y, x)]
    line_peers = [x_peers, y_peers]
    before = [lax.rem(place[1] + SIDE - 1, SIDE) for place in mine]
    after = [lax.rem(place[1] + 1, SIDE) for place in mine]
    opposite = [lax.rem(place[1] + 2, SIDE) for place in mine]

    def line(ref, half, across):
        return ref.at[across] if half == 0 else ref.at[:, across]

    def spot(ref, half, on_line, across):
        row, column = chip_at(half, on_line, across)
        return ref.at[row, column]

    def to_chip(core, half, on_line, across):
        return device(core, *chip_at(half, on_line, across))

    def first_step(source, t, g, half, core):
        target = gathered.at[t, g, half, y, x]
        to_recv, to_send = recv_sem.at[0, t, g], send_sem.at[0, t, g]
        on_line, across = mine[half]
        for peer in line_peers[half]:
            send(source, target, to_send, to_recv, to_chip(core, half, peer, across))
        send(source, target, to_send, to_recv, to_chip(core, half, on_line, opposite[half]))

    for group in range(GROUPS):
        for half in range(2):
            block = tokens_ref.at[:, pl.ds((2 * group + half) * lanes, lanes)]
            pltpu.make_async_copy(block, gathered.at[0, group, half, y, x], recv_sem.at[0, 0, group]).start()
            first_step(block, 0, group, half, section)
        if group == 0:
            pltpu.make_async_copy(gain_own, gain_all.at[y, x], gain_recv.at[0]).start()
            for peer in y_peers:
                send(gain_own, gain_all.at[y, x], gain_send.at[0], gain_recv.at[0], device(section, peer, x))

    expert = chip // 2
    for t in range(STOPS):
        for g in range(GROUPS):
            span = pl.ds(2 * g * lanes, 2 * lanes)
            ids, logits = ids_ref[t, :, span], logits_ref[t, :, span]
            one = jax.nn.sigmoid(logits[0:1] - logits[1:2])
            two = jax.nn.sigmoid(logits[1:2] - logits[0:1])
            weight[t, g] = jnp.where(ids[0:1] == expert, one, 0.0) + jnp.where(ids[1:2] == expert, two, 0.0)

    def spread(t, g):
        wait_blocks(recv_sem.at[0, t, g], 10)
        to_recv, to_send = recv_sem.at[1, t, g], send_sem.at[1, t, g]
        for half in range(2):
            on_line, across = mine[half]
            own_line = line(gathered.at[t, g, half], half, across)
            for beside in (before[half], after[half]):
                send(own_line, own_line, to_send, to_recv, to_chip(section, half, on_line, beside))
        for half in range(2):
            on_line, across = mine[half]
            far = spot(gathered.at[t, g, half], half, on_line, opposite[half])
            for peer in line_peers[half]:
                send(far, far, to_send, to_recv, to_chip(section, half, peer, across))

    def compute(t, g):
        wait_blocks(recv_sem.at[1, t, g], 22)
        acts = jnp.concatenate(
            [gathered[t, g, half].reshape(D, lanes) for half in range(2)], axis=1
        ).astype(jnp.float32)
        inverse = lax.rsqrt(jnp.sum(acts * acts, axis=0, keepdims=True) / D + 1e-05)
        gain = gain_all[...].reshape(D, 128).astype(jnp.float32)
        gain = jnp.concatenate([gain] * (2 * lanes // 128), axis=1)
        normed = (acts * inverse * gain).astype(jnp.bfloat16)
        pieces = []
        for start in range(0, D, PIECE):
            gate_val = jnp.dot(gate_t[start:start + PIECE], normed, preferred_element_type=jnp.float32)
            up_val = jnp.dot(up_t[start:start + PIECE], normed, preferred_element_type=jnp.float32)
            pieces.append((jax.nn.silu(gate_val) * up_val).astype(jnp.bfloat16))
        hidden = jnp.concatenate(pieces, axis=0)
        outcome = jnp.dot(down_t[...], hidden, preferred_element_type=jnp.float32)
        outcome = (outcome * weight[t, g]).astype(jnp.bfloat16)
        for half in range(2):
            partial[t, g, half] = outcome[:, half * lanes:(half + 1) * lanes].reshape(SIDE, SIDE, SLICE, lanes)
        to_recv, to_send = recv_sem.at[2, t, g], send_sem.at[2, t, g]
        for half in range(2):
            on_line, across = mine[half]
            for beside, slot in ((before[half], 1), (after[half], 0)):
                send(line(partial.at[t, g, half], half, beside), returned.at[t, g, half, slot], to_send, to_recv,
                     to_chip(section, half, on_line, beside))
        for half in range(2):
            on_line, across = mine[half]
            for peer in line_peers[half]:
                send(spot(partial.at[t, g, half], half, peer, opposite[half]), returned.at[t, g, half, 2, on_line],
                     to_send, to_recv, to_chip(section, half, peer, across))

    def collect(t, g):
        wait_blocks(recv_sem.at[2, t, g], 22)
        to_recv, to_send = recv_sem.at[3, t, g], send_sem.at[3, t, g]
        for half in range(2):
            on_line, across = mine[half]
            total = line(partial.at[t, g, half], half, across)[...].astype(jnp.float32)
            total = total + returned[t, g, half, 0].astype(jnp.float32) + returned[t, g, half, 1].astype(jnp.float32)
            summed[t, g, half, 0:SIDE] = total.astype(jnp.bfloat16)
            total = spot(partial.at[t, g, half], half, on_line, opposite[half])[...].astype(jnp.float32)
            for peer in line_peers[half]:
                total = total + returned[t, g, half, 2, peer].astype(jnp.float32)
            summed[t, g, half, SIDE] = total.astype(jnp.bfloat16)
            for peer in line_peers[half]:
                send(summed.at[t, g, half, peer], last.at[t, g, half, on_line], to_send, to_recv,
                     to_chip(section, half, peer, across))
            send(summed.at[t, g, half, SIDE], last.at[t, g, half, SIDE], to_send, to_recv,
                 to_chip(section, half, on_line, opposite[half]))

    def finish(t, g):
        wait_blocks(recv_sem.at[3, t, g], 8)
        for half in range(2):
            on_line, across = mine[half]
            total = summed[t, g, half, on_line].astype(jnp.float32) + last[t, g, half, SIDE].astype(jnp.float32)
            for peer in line_peers[half]:
                total = total + last[t, g, half, peer].astype(jnp.float32)
            total = gathered[t, g, half, y, x].astype(jnp.float32) + total
            held[t, g, half] = total.astype(jnp.bfloat16)

        @pl.when(t < STOPS - 1)
        def _():
            later = jnp.minimum(t + 1, STOPS - 1)
            for half in range(2):
                block = held.at[t, g, half]
                first_step(block, later, g, half, other)
                send(block, gathered.at[later, g, half, y, x], send_sem.at[0, later, g], recv_sem.at[0, later, g],
                     device(other, y, x))

        @pl.when(t == STOPS - 1)
        def _():
            send(held.at[t, g], final.at[g], final_send.at[g], final_recv.at[g], device(other, y, x))

    def each_group(stage, t):
        def one(g, carry):
            stage(t, g)
            return carry
        lax.fori_loop(0, GROUPS, one, 0)

    each_group(spread, 0)
    wait_gain(gain_recv.at[0], 4)
    for peer in x_peers:
        send(gain_all.at[:, x], gain_all.at[:, x], gain_send.at[1], gain_recv.at[1], device(section, y, peer))
    for i, target in enumerate((gate_t, up_t, down_t)):
        loads[i].wait()
        target[...] = raw[i].T
    wait_gain(gain_recv.at[1], 12)

    def stop(t, carry):
        each_group(compute, t)
        each_group(collect, t)
        each_group(finish, t)

        @pl.when(t < STOPS - 1)
        def _():
            each_group(spread, jnp.minimum(t + 1, STOPS - 1))
        return carry

    lax.fori_loop(0, STOPS, stop, 0)

    def settle(t, carry):
        for g in range(GROUPS):
            for k, blocks in ((1, 22), (2, 22), (3, 8)):
                wait_blocks(send_sem.at[k, t, g], blocks)

            @pl.when(t == 0)
            def _():
                wait_blocks(send_sem.at[0, 0, g], 8)

            @pl.when(t > 0)
            def _():
                wait_blocks(send_sem.at[0, t, g], 10)
        return carry

    lax.fori_loop(0, STOPS, settle, 0)
    wait_gain(gain_send.at[0], 3)
    wait_gain(gain_send.at[1], 12)
    for g in range(GROUPS):
        wait_blocks(final_send.at[g], 2)
        wait_blocks(final_recv.at[g], 2)
        for half in range(2):
            out_ref[:, (2 * g + half) * lanes:(2 * g + half + 1) * lanes] = final[g, half]


def per_device(tokens, norm_gain, w_gate, w_up, w_down, expert_ids, gate_logits):
    rows, width = tokens.shape[1:]
    lanes = rows // (2 * GROUPS)
    block = (STOPS, GROUPS, 2)
    vmem = pl.BlockSpec(memory_space=pltpu.VMEM)
    out = pl.pallas_call(
        kernel,
        out_shape=jax.ShapeDtypeStruct((width, rows), jnp.bfloat16),
        in_specs=[vmem] * 4 + [pl.BlockSpec(memory_space=pl.ANY)] * 3,
        out_specs=vmem,
        scratch_shapes=[
            pltpu.VMEM(block + (SIDE, SIDE, width, lanes), jnp.bfloat16),
            pltpu.VMEM(block + (SIDE, SIDE, width, lanes), jnp.bfloat16),
            pltpu.VMEM(block + (3, SIDE, width, lanes), jnp.bfloat16),
            pltpu.VMEM(block + (SIDE + 1, width, lanes), jnp.bfloat16),
            pltpu.VMEM(block + (SIDE + 1, width, lanes), jnp.bfloat16),
            pltpu.VMEM(block + (width, lanes), jnp.bfloat16),
            pltpu.VMEM((GROUPS, 2, width, lanes), jnp.bfloat16),
            pltpu.VMEM((width, 128), jnp.bfloat16),
            pltpu.VMEM((SIDE, SIDE, width, 128), jnp.bfloat16),
            pltpu.VMEM((STOPS, GROUPS, 1, 2 * lanes), jnp.float32),
            pltpu.VMEM((D, D), jnp.bfloat16),
            pltpu.VMEM((D, D), jnp.bfloat16),
            pltpu.VMEM((D, D), jnp.bfloat16),
            pltpu.VMEM((3, D, D), jnp.bfloat16),
            pltpu.SemaphoreType.DMA((4, STOPS, GROUPS)),
            pltpu.SemaphoreType.DMA((4, STOPS, GROUPS)),
            pltpu.SemaphoreType.DMA((GROUPS,)),
            pltpu.SemaphoreType.DMA((GROUPS,)),
            pltpu.SemaphoreType.DMA((2,)),
            pltpu.SemaphoreType.DMA((2,)),
            pltpu.SemaphoreType.DMA((3,)),
        ],
        compiler_params=pltpu.CompilerParams(
            collective_id=0, has_side_effects=True, vmem_limit_bytes=56 << 20
        ),
    )(
        tokens[0].T, norm_gain, expert_ids[0].transpose(0, 2, 1), gate_logits[0].transpose(0, 2, 1),
        w_gate[0], w_up[0], w_down[0],
    )
    return out.T[None]


def solution(mesh):
    placed = (
        P("section", "dp", "expert"),
        P("section", "expert"),
        P("section", None, "expert"),
        P("section", None, "expert"),
        P("section", "expert", None),
        P("section", None, "dp", None),
        P("section", None, "dp", None),
    )
    return jax.shard_map(
        per_device,
        mesh=mesh,
        in_specs=placed,
        out_specs=P("section", "dp", "expert"),
        check_vma=False,
    )
```

```python
import jax
import jax.numpy as jnp
from jax import lax
from jax.experimental import pallas as pl
from jax.experimental.pallas import tpu as pltpu
from jax.sharding import PartitionSpec as P

D = 768
STOPS = 4
GROUPS = 4
SIDE = 4
SLICE = 48
PIECE = 256
MESH = pl.DeviceIdType.MESH


def kernel(
    tokens_ref, gain_in, ids_in, logits_in, gate_ref, up_ref, down_ref,
    out_ref,
    gathered, partial, returned, summed, last, held, final, gain_own, gain_all, weight,
    gate_t, up_t, down_t, raw, gain_ref, ids_ref, logits_ref,
    recv_sem, send_sem, gain_recv, gain_send, load_sem, out_sem,
):
    section = lax.axis_index("section")
    chip = lax.axis_index("expert")
    plane = lax.axis_index("dp")
    y, x = chip // SIDE, lax.rem(chip, SIDE)
    lanes = gathered.shape[-1]

    def device(core, row, column):
        return (core, row * SIDE + column, plane)

    other = 1 - section
    y_peers = [lax.rem(y + step, SIDE) for step in range(1, SIDE)]
    x_peers = [lax.rem(x + step, SIDE) for step in range(1, SIDE)]

    barrier = pltpu.get_barrier_semaphore()
    partners = [device(other, y, x)]
    for core in (section, other):
        partners += [device(core, row, x) for row in y_peers]
        partners += [device(core, y, column) for column in x_peers]
    for partner in partners:
        pl.semaphore_signal(barrier, inc=1, device_id=partner, device_id_type=MESH)
    loads = [
        pltpu.make_async_copy(source, target, load_sem.at[i])
        for i, (source, target) in enumerate((
            (gain_in, gain_ref), (ids_in, ids_ref), (logits_in, logits_ref),
            (gate_ref, raw.at[0]), (up_ref, raw.at[1]), (down_ref, raw.at[2]),
        ))
    ]
    for load in loads:
        load.start()
    loads[0].wait()
    gain_row = jnp.broadcast_to(gain_ref[...].astype(jnp.float32), (128, SLICE))
    gain_own[...] = gain_row.T.astype(jnp.bfloat16)
    pl.semaphore_wait(barrier, len(partners))

    def send(source, target, send_at, recv_at, to):
        pltpu.make_async_remote_copy(
            src_ref=source, dst_ref=target, send_sem=send_at, recv_sem=recv_at,
            device_id=to, device_id_type=MESH,
        ).start()

    def wait_blocks(sem, blocks):
        view = gathered.at[0, 0].reshape(2 * SIDE * SIDE, SLICE, lanes).at[pl.ds(0, blocks)]
        pltpu.make_async_copy(view, view, sem).wait()

    def wait_gain(sem, blocks):
        view = gain_all.reshape(SIDE * SIDE, SLICE, 128).at[pl.ds(0, blocks)]
        pltpu.make_async_copy(view, view, sem).wait()

    def chip_at(half, on_line, across):
        return (across, on_line) if half == 0 else (on_line, across)

    mine = [(x, y), (y, x)]
    line_peers = [[peers[1], peers[0], peers[2]] for peers in (x_peers, y_peers)]
    before = [lax.rem(place[1] + SIDE - 1, SIDE) for place in mine]
    after = [lax.rem(place[1] + 1, SIDE) for place in mine]
    opposite = [lax.rem(place[1] + 2, SIDE) for place in mine]

    def line(ref, half, across):
        return ref.at[across] if half == 0 else ref.at[:, across]

    def spot(ref, half, on_line, across):
        row, column = chip_at(half, on_line, across)
        return ref.at[row, column]

    def to_chip(core, half, on_line, across):
        return device(core, *chip_at(half, on_line, across))

    def first_step(source, t, g, half, core):
        target = gathered.at[t, g, half, y, x]
        to_recv, to_send = recv_sem.at[0, t, g], send_sem.at[0]
        on_line, across = mine[half]
        send(source, target, to_send, to_recv, to_chip(core, half, on_line, opposite[half]))
        for peer in line_peers[half]:
            send(source, target, to_send, to_recv, to_chip(core, half, peer, across))

    for group in range(GROUPS):
        for half in range(2):
            block = tokens_ref.at[:, pl.ds((2 * group + half) * lanes, lanes)]
            pltpu.make_async_copy(block, gathered.at[0, group, half, y, x], recv_sem.at[0, 0, group]).start()
            first_step(block, 0, group, half, section)
        if group == 0:
            pltpu.make_async_copy(gain_own, gain_all.at[y, x], gain_recv.at[0]).start()
            for peer in y_peers:
                send(gain_own, gain_all.at[y, x], gain_send.at[0], gain_recv.at[0], device(section, peer, x))

    expert = chip // 2
    loads[1].wait()
    loads[2].wait()
    for t in range(STOPS):
        for g in range(GROUPS):
            span = pl.ds(2 * g * lanes, 2 * lanes)
            ids, logits = ids_ref[t, :, span], logits_ref[t, :, span]
            one = jax.nn.sigmoid(logits[0:1] - logits[1:2])
            two = jax.nn.sigmoid(logits[1:2] - logits[0:1])
            weight[t, g] = jnp.where(ids[0:1] == expert, one, 0.0) + jnp.where(ids[1:2] == expert, two, 0.0)

    def spread(t, g):
        wait_blocks(recv_sem.at[0, t, g], 10)
        to_recv, to_send = recv_sem.at[1, t, g], send_sem.at[1]
        for half in range(2):
            on_line, across = mine[half]
            far = spot(gathered.at[t, g, half], half, on_line, opposite[half])
            for peer in line_peers[half]:
                send(far, far, to_send, to_recv, to_chip(section, half, peer, across))
        for side in (before, after):
            for half in range(2):
                own_line = line(gathered.at[t, g, half], half, mine[half][1])
                send(own_line, own_line, to_send, to_recv, to_chip(section, half, mine[half][0], side[half]))

    def compute(t, g):
        wait_blocks(recv_sem.at[1, t, g], 22)
        acts = jnp.concatenate(
            [gathered[t, g, half].reshape(D, lanes) for half in range(2)], axis=1
        ).astype(jnp.float32)
        inverse = lax.rsqrt(jnp.sum(acts * acts, axis=0, keepdims=True) / D + 1e-05)
        gain = gain_all[...].reshape(D, 128).astype(jnp.float32)
        gain = jnp.concatenate([gain] * (2 * lanes // 128), axis=1)
        normed = (acts * inverse * gain).astype(jnp.bfloat16)
        pieces = []
        for start in range(0, D, PIECE):
            gate_val = jnp.dot(gate_t[start:start + PIECE], normed, preferred_element_type=jnp.float32)
            up_val = jnp.dot(up_t[start:start + PIECE], normed, preferred_element_type=jnp.float32)
            pieces.append((jax.nn.silu(gate_val) * up_val).astype(jnp.bfloat16))
        hidden = jnp.concatenate(pieces, axis=0)
        outcome = jnp.dot(down_t[...], hidden, preferred_element_type=jnp.float32)
        outcome = (outcome * weight[t, g]).astype(jnp.bfloat16)
        for half in range(2):
            partial[t, g, half] = outcome[:, half * lanes:(half + 1) * lanes].reshape(SIDE, SIDE, SLICE, lanes)
        to_recv, to_send = recv_sem.at[2, t, g], send_sem.at[2]
        for half in range(2):
            on_line, across = mine[half]
            for peer in line_peers[half]:
                send(spot(partial.at[t, g, half], half, peer, opposite[half]), returned.at[t, g, half, 2, on_line],
                     to_send, to_recv, to_chip(section, half, peer, across))
        for side, slot in ((before, 1), (after, 0)):
            for half in range(2):
                send(line(partial.at[t, g, half], half, side[half]), returned.at[t, g, half, slot], to_send, to_recv,
                     to_chip(section, half, mine[half][0], side[half]))

    def collect(t, g):
        wait_blocks(recv_sem.at[2, t, g], 22)
        core = lax.rem(section + t // (STOPS - 1), 2)
        to_recv, to_send = recv_sem.at[3, t, g], send_sem.at[3]
        for half in range(2):
            on_line, across = mine[half]
            total = line(partial.at[t, g, half], half, across)[...].astype(jnp.float32)
            total = total + returned[t, g, half, 0].astype(jnp.float32) + returned[t, g, half, 1].astype(jnp.float32)
            summed[t, g, half, 0:SIDE] = total.astype(jnp.bfloat16)
            total = spot(partial.at[t, g, half], half, on_line, opposite[half])[...].astype(jnp.float32)
            for peer in line_peers[half]:
                total = total + returned[t, g, half, 2, peer].astype(jnp.float32)
            summed[t, g, half, SIDE] = total.astype(jnp.bfloat16)
            for peer in line_peers[half]:
                send(summed.at[t, g, half, peer], last.at[t, g, half, on_line], to_send, to_recv,
                     to_chip(core, half, peer, across))
            send(summed.at[t, g, half, SIDE], last.at[t, g, half, SIDE], to_send, to_recv,
                 to_chip(core, half, on_line, opposite[half]))

            @pl.when(t == STOPS - 1)
            def _(half=half, on_line=on_line):
                send(summed.at[t, g, half, on_line], last.at[t, g, half, on_line], to_send, to_recv, device(other, y, x))
                send(gathered.at[t, g, half, y, x], final.at[g, half], to_send, to_recv, device(other, y, x))

    def finish(t, g):
        @pl.when(t < STOPS - 1)
        def _():
            wait_blocks(recv_sem.at[3, t, g], 8)
            later = jnp.minimum(t + 1, STOPS - 1)
            for half in range(2):
                on_line, across = mine[half]
                total = summed[t, g, half, on_line].astype(jnp.float32) + last[t, g, half, SIDE].astype(jnp.float32)
                for peer in line_peers[half]:
                    total = total + last[t, g, half, peer].astype(jnp.float32)
                total = gathered[t, g, half, y, x].astype(jnp.float32) + total
                held[t, g, half] = total.astype(jnp.bfloat16)
                block = held.at[t, g, half]
                first_step(block, later, g, half, other)
                send(block, gathered.at[later, g, half, y, x], send_sem.at[0], recv_sem.at[0, later, g],
                     device(other, y, x))

        @pl.when(t == STOPS - 1)
        def _():
            wait_blocks(recv_sem.at[3, t, g], 12)
            for half in range(2):
                total = jnp.sum(last[t, g, half].astype(jnp.float32), axis=0)
                total = final[g, half].astype(jnp.float32) + total
                held[t, g, half] = total.astype(jnp.bfloat16)
                to_out(t, g, half).start()

    def to_out(t, g, half):
        span = pl.ds(pl.multiple_of((2 * g + half) * lanes, lanes), lanes)
        return pltpu.make_async_copy(held.at[t, g, half], out_ref.at[:, span], out_sem.at[g, half])

    def each_group(stage, t):
        def one(g, carry):
            stage(t, g)
            return carry
        lax.fori_loop(0, GROUPS, one, 0)

    each_group(spread, 0)
    wait_gain(gain_recv.at[0], 4)
    for peer in x_peers:
        send(gain_all.at[:, x], gain_all.at[:, x], gain_send.at[1], gain_recv.at[1], device(section, y, peer))
    for i, target in enumerate((gate_t, up_t, down_t)):
        loads[i + 3].wait()
        target[...] = raw[i].T
    wait_gain(gain_recv.at[1], 12)

    def stop(t, carry):
        each_group(compute, t)
        each_group(collect, t)
        each_group(finish, t)

        @pl.when(t < STOPS - 1)
        def _():
            each_group(spread, jnp.minimum(t + 1, STOPS - 1))
        return carry

    lax.fori_loop(0, STOPS, stop, 0)

    steps = STOPS * GROUPS
    sent = (8 * GROUPS + 10 * (steps - GROUPS), 22 * steps, 22 * steps, 8 * (steps - GROUPS) + 12 * GROUPS)
    for k, blocks in enumerate(sent):
        view = gathered.reshape(steps * 2 * SIDE * SIDE, SLICE, lanes).at[pl.ds(0, blocks)]
        pltpu.make_async_copy(view, view, send_sem.at[k]).wait()
    wait_gain(gain_send.at[0], 3)
    wait_gain(gain_send.at[1], 12)
    for g in range(GROUPS):
        for half in range(2):
            to_out(STOPS - 1, g, half).wait()


def per_device(tokens, norm_gain, w_gate, w_up, w_down, expert_ids, gate_logits):
    rows, width = tokens.shape[1:]
    lanes = rows // (2 * GROUPS)
    block = (STOPS, GROUPS, 2)
    anywhere = pl.BlockSpec(memory_space=pl.ANY)
    out = pl.pallas_call(
        kernel,
        out_shape=jax.ShapeDtypeStruct((width, rows), jnp.bfloat16),
        in_specs=[anywhere] * 7,
        out_specs=anywhere,
        scratch_shapes=[
            pltpu.VMEM(block + (SIDE, SIDE, width, lanes), jnp.bfloat16),
            pltpu.VMEM(block + (SIDE, SIDE, width, lanes), jnp.bfloat16),
            pltpu.VMEM(block + (3, SIDE, width, lanes), jnp.bfloat16),
            pltpu.VMEM(block + (SIDE + 1, width, lanes), jnp.bfloat16),
            pltpu.VMEM(block + (SIDE + 1, width, lanes), jnp.bfloat16),
            pltpu.VMEM(block + (width, lanes), jnp.bfloat16),
            pltpu.VMEM((GROUPS, 2, width, lanes), jnp.bfloat16),
            pltpu.VMEM((width, 128), jnp.bfloat16),
            pltpu.VMEM((SIDE, SIDE, width, 128), jnp.bfloat16),
            pltpu.VMEM((STOPS, GROUPS, 1, 2 * lanes), jnp.float32),
            pltpu.VMEM((D, D), jnp.bfloat16),
            pltpu.VMEM((D, D), jnp.bfloat16),
            pltpu.VMEM((D, D), jnp.bfloat16),
            pltpu.VMEM((3, D, D), jnp.bfloat16),
            pltpu.VMEM((1, width), jnp.bfloat16),
            pltpu.VMEM((STOPS, 2, rows), jnp.int32),
            pltpu.VMEM((STOPS, 2, rows), jnp.float32),
            pltpu.SemaphoreType.DMA((4, STOPS, GROUPS)),
            pltpu.SemaphoreType.DMA((4,)),
            pltpu.SemaphoreType.DMA((2,)),
            pltpu.SemaphoreType.DMA((2,)),
            pltpu.SemaphoreType.DMA((6,)),
            pltpu.SemaphoreType.DMA((GROUPS, 2)),
        ],
        compiler_params=pltpu.CompilerParams(
            collective_id=0, has_side_effects=True, vmem_limit_bytes=56 << 20
        ),
    )(
        tokens[0].T, norm_gain, expert_ids[0].transpose(0, 2, 1), gate_logits[0].transpose(0, 2, 1),
        w_gate[0], w_up[0], w_down[0],
    )
    return out.T[None]


def solution(mesh):
    placed = (
        P("section", "dp", "expert"),
        P("section", "expert"),
        P("section", None, "expert"),
        P("section", None, "expert"),
        P("section", "expert", None),
        P("section", None, "dp", None),
        P("section", None, "dp", None),
    )
    return jax.shard_map(
        per_device,
        mesh=mesh,
        in_specs=placed,
        out_specs=P("section", "dp", "expert"),
        check_vma=False,
    )
```

```python
import jax
import jax.numpy as jnp
from jax import lax
from jax.experimental import pallas as pl
from jax.experimental.pallas import tpu as pltpu
from jax.sharding import PartitionSpec as P

D = 768
STOPS = 4
GROUPS = 4
SIDE = 4
SLICE = 48
PIECE = 256
MESH = pl.DeviceIdType.MESH


def kernel(
    tokens_ref, gain_in, ids_in, logits_in, gate_ref, up_ref, down_ref,
    out_ref,
    gathered, partial, returned, summed, last, held, final, gain_own, gain_all, weight,
    gate_t, up_t, down_t, raw, gain_ref, ids_ref, logits_ref,
    recv_sem, send_sem, gain_recv, gain_send, load_sem, out_sem,
):
    section = lax.axis_index("section")
    chip = lax.axis_index("expert")
    plane = lax.axis_index("dp")
    y, x = chip // SIDE, lax.rem(chip, SIDE)
    lanes = gathered.shape[-1]

    def device(core, row, column):
        return (core, row * SIDE + column, plane)

    other = 1 - section
    y_peers = [lax.rem(y + step, SIDE) for step in range(1, SIDE)]
    x_peers = [lax.rem(x + step, SIDE) for step in range(1, SIDE)]

    barrier = pltpu.get_barrier_semaphore()
    partners = [device(other, y, x)]
    for core in (section, other):
        partners += [device(core, row, x) for row in y_peers]
        partners += [device(core, y, column) for column in x_peers]
    for partner in partners:
        pl.semaphore_signal(barrier, inc=1, device_id=partner, device_id_type=MESH)
    loads = [
        pltpu.make_async_copy(source, target, load_sem.at[i])
        for i, (source, target) in enumerate((
            (gain_in, gain_ref), (ids_in, ids_ref), (logits_in, logits_ref),
            (gate_ref, raw.at[0]), (up_ref, raw.at[1]), (down_ref, raw.at[2]),
        ))
    ]
    for load in loads:
        load.start()
    loads[0].wait()
    gain_row = jnp.broadcast_to(gain_ref[...].astype(jnp.float32), (128, SLICE))
    gain_own[...] = gain_row.T.astype(jnp.bfloat16)
    pl.semaphore_wait(barrier, len(partners))

    def send(source, target, send_at, recv_at, to):
        pltpu.make_async_remote_copy(
            src_ref=source, dst_ref=target, send_sem=send_at, recv_sem=recv_at,
            device_id=to, device_id_type=MESH,
        ).start()

    def wait_blocks(sem, blocks):
        view = gathered.at[0, 0].reshape(2 * SIDE * SIDE, SLICE, lanes).at[pl.ds(0, blocks)]
        pltpu.make_async_copy(view, view, sem).wait()

    def wait_gain(sem, blocks):
        view = gain_all.reshape(SIDE * SIDE, SLICE, 128).at[pl.ds(0, blocks)]
        pltpu.make_async_copy(view, view, sem).wait()

    def chip_at(half, on_line, across):
        return (across, on_line) if half == 0 else (on_line, across)

    mine = [(x, y), (y, x)]
    line_peers = [[peers[1], peers[0], peers[2]] for peers in (x_peers, y_peers)]
    before = [lax.rem(place[1] + SIDE - 1, SIDE) for place in mine]
    after = [lax.rem(place[1] + 1, SIDE) for place in mine]
    opposite = [lax.rem(place[1] + 2, SIDE) for place in mine]

    def line(ref, half, across):
        return ref.at[across] if half == 0 else ref.at[:, across]

    def spot(ref, half, on_line, across):
        row, column = chip_at(half, on_line, across)
        return ref.at[row, column]

    def to_chip(core, half, on_line, across):
        return device(core, *chip_at(half, on_line, across))

    def first_step(source, t, g, half, core):
        target = gathered.at[t, g, half, y, x]
        to_recv, to_send = recv_sem.at[0, t, g], send_sem.at[0]
        on_line, across = mine[half]
        send(source, target, to_send, to_recv, to_chip(core, half, on_line, opposite[half]))
        for peer in line_peers[half]:
            send(source, target, to_send, to_recv, to_chip(core, half, peer, across))
        for side in (before, after):
            send(source, target, to_send, to_recv, to_chip(core, half, on_line, side[half]))

    for group in range(GROUPS):
        for half in range(2):
            block = tokens_ref.at[:, pl.ds((2 * group + half) * lanes, lanes)]
            pltpu.make_async_copy(block, gathered.at[0, group, half, y, x], recv_sem.at[0, 0, group]).start()
            first_step(block, 0, group, half, section)
        if group == 0:
            pltpu.make_async_copy(gain_own, gain_all.at[y, x], gain_recv.at[0]).start()
            for peer in y_peers:
                send(gain_own, gain_all.at[y, x], gain_send.at[0], gain_recv.at[0], device(section, peer, x))

    expert = chip // 2
    loads[1].wait()
    loads[2].wait()
    for t in range(STOPS):
        for g in range(GROUPS):
            span = pl.ds(2 * g * lanes, 2 * lanes)
            ids, logits = ids_ref[t, :, span], logits_ref[t, :, span]
            one = jax.nn.sigmoid(logits[0:1] - logits[1:2])
            two = jax.nn.sigmoid(logits[1:2] - logits[0:1])
            weight[t, g] = jnp.where(ids[0:1] == expert, one, 0.0) + jnp.where(ids[1:2] == expert, two, 0.0)

    def spread(t, g):
        wait_blocks(recv_sem.at[0, t, g], 14)
        to_recv, to_send = recv_sem.at[1, t, g], send_sem.at[1]
        for half in range(2):
            on_line, across = mine[half]
            far = spot(gathered.at[t, g, half], half, on_line, opposite[half])
            for peer in line_peers[half]:
                send(far, far, to_send, to_recv, to_chip(section, half, peer, across))
        for side in (before, after):
            for half in range(2):
                on_line, across = mine[half]
                for peer in line_peers[half]:
                    block = spot(gathered.at[t, g, half], half, peer, across)
                    send(block, block, to_send, to_recv, to_chip(section, half, on_line, side[half]))

    def compute(t, g):
        wait_blocks(recv_sem.at[1, t, g], 18)
        acts = jnp.concatenate(
            [gathered[t, g, half].reshape(D, lanes) for half in range(2)], axis=1
        ).astype(jnp.float32)
        inverse = lax.rsqrt(jnp.sum(acts * acts, axis=0, keepdims=True) / D + 1e-05)
        gain = gain_all[...].reshape(D, 128).astype(jnp.float32)
        gain = jnp.concatenate([gain] * (2 * lanes // 128), axis=1)
        normed = (acts * inverse * gain).astype(jnp.bfloat16)
        pieces = []
        for start in range(0, D, PIECE):
            gate_val = jnp.dot(gate_t[start:start + PIECE], normed, preferred_element_type=jnp.float32)
            up_val = jnp.dot(up_t[start:start + PIECE], normed, preferred_element_type=jnp.float32)
            pieces.append((jax.nn.silu(gate_val) * up_val).astype(jnp.bfloat16))
        hidden = jnp.concatenate(pieces, axis=0)
        outcome = jnp.dot(down_t[...], hidden, preferred_element_type=jnp.float32)
        outcome = (outcome * weight[t, g]).astype(jnp.bfloat16)
        for half in range(2):
            partial[t, g, half] = outcome[:, half * lanes:(half + 1) * lanes].reshape(SIDE, SIDE, SLICE, lanes)
        to_recv, to_send = recv_sem.at[2, t, g], send_sem.at[2]
        for half in range(2):
            on_line, across = mine[half]
            for peer in line_peers[half]:
                send(spot(partial.at[t, g, half], half, peer, opposite[half]), returned.at[t, g, half, 2, on_line],
                     to_send, to_recv, to_chip(section, half, peer, across))
        for side, slot in ((before, 1), (after, 0)):
            for half in range(2):
                on_line, across = mine[half]
                for peer in line_peers[half]:
                    send(spot(partial.at[t, g, half], half, peer, side[half]), returned.at[t, g, half, slot, peer],
                         to_send, to_recv, to_chip(section, half, on_line, side[half]))

    def collect(t, g):
        wait_blocks(recv_sem.at[2, t, g], 18)
        core = lax.rem(section + t // (STOPS - 1), 2)
        to_recv, to_send = recv_sem.at[3, t, g], send_sem.at[3]
        for half in range(2):
            on_line, across = mine[half]
            total = spot(partial.at[t, g, half], half, on_line, opposite[half])[...].astype(jnp.float32)
            for peer in line_peers[half]:
                total = total + returned[t, g, half, 2, peer].astype(jnp.float32)
            summed[t, g, half, SIDE] = total.astype(jnp.bfloat16)
            send(summed.at[t, g, half, SIDE], last.at[t, g, half, SIDE], to_send, to_recv,
                 to_chip(core, half, on_line, opposite[half]))
            for peer in line_peers[half]:
                total = spot(partial.at[t, g, half], half, peer, across)[...].astype(jnp.float32)
                for slot in range(2):
                    total = total + returned[t, g, half, slot, peer].astype(jnp.float32)
                summed[t, g, half, peer] = total.astype(jnp.bfloat16)
                send(summed.at[t, g, half, peer], last.at[t, g, half, on_line], to_send, to_recv,
                     to_chip(core, half, peer, across))
            for side, slot in ((before, SIDE + 2), (after, SIDE + 1)):
                send(spot(partial.at[t, g, half], half, on_line, side[half]), last.at[t, g, half, slot], to_send, to_recv,
                     to_chip(core, half, on_line, side[half]))

            @pl.when(t == STOPS - 1)
            def _(half=half, on_line=on_line):
                send(partial.at[t, g, half, y, x], last.at[t, g, half, on_line], to_send, to_recv, device(other, y, x))
                send(gathered.at[t, g, half, y, x], final.at[g, half], to_send, to_recv, device(other, y, x))

    def finish(t, g):
        @pl.when(t < STOPS - 1)
        def _():
            wait_blocks(recv_sem.at[3, t, g], 12)
            later = jnp.minimum(t + 1, STOPS - 1)
            for half in range(2):
                on_line, across = mine[half]
                total = partial[t, g, half, y, x].astype(jnp.float32)
                for peer in line_peers[half] + [SIDE, SIDE + 1, SIDE + 2]:
                    total = total + last[t, g, half, peer].astype(jnp.float32)
                total = gathered[t, g, half, y, x].astype(jnp.float32) + total
                held[t, g, half] = total.astype(jnp.bfloat16)
                block = held.at[t, g, half]
                first_step(block, later, g, half, other)
                send(block, gathered.at[later, g, half, y, x], send_sem.at[0], recv_sem.at[0, later, g],
                     device(other, y, x))

        @pl.when(t == STOPS - 1)
        def _():
            wait_blocks(recv_sem.at[3, t, g], 16)
            for half in range(2):
                total = jnp.sum(last[t, g, half].astype(jnp.float32), axis=0)
                total = final[g, half].astype(jnp.float32) + total
                held[t, g, half] = total.astype(jnp.bfloat16)
                to_out(t, g, half).start()

    def to_out(t, g, half):
        span = pl.ds(pl.multiple_of((2 * g + half) * lanes, lanes), lanes)
        return pltpu.make_async_copy(held.at[t, g, half], out_ref.at[:, span], out_sem.at[g, half])

    def each_group(stage, t):
        def one(g, carry):
            stage(t, g)
            return carry
        lax.fori_loop(0, GROUPS, one, 0)

    for g in range(GROUPS):
        spread(0, g)
        if g == 0:
            wait_gain(gain_recv.at[0], 4)
            for peer in x_peers:
                send(gain_all.at[:, x], gain_all.at[:, x], gain_send.at[1], gain_recv.at[1], device(section, y, peer))
    for i, target in enumerate((gate_t, up_t, down_t)):
        loads[i + 3].wait()
        target[...] = raw[i].T
    wait_gain(gain_recv.at[1], 12)

    def stop(t, carry):
        each_group(compute, t)
        each_group(collect, t)
        each_group(finish, t)

        @pl.when(t < STOPS - 1)
        def _():
            each_group(spread, jnp.minimum(t + 1, STOPS - 1))
        return carry

    lax.fori_loop(0, STOPS, stop, 0)

    steps = STOPS * GROUPS
    sent = (12 * GROUPS + 14 * (steps - GROUPS), 18 * steps, 18 * steps, 12 * (steps - GROUPS) + 16 * GROUPS)
    for k, blocks in enumerate(sent):
        view = gathered.reshape(steps * 2 * SIDE * SIDE, SLICE, lanes).at[pl.ds(0, blocks)]
        pltpu.make_async_copy(view, view, send_sem.at[k]).wait()
    wait_gain(gain_send.at[0], 3)
    wait_gain(gain_send.at[1], 12)
    for g in range(GROUPS):
        for half in range(2):
            to_out(STOPS - 1, g, half).wait()


def per_device(tokens, norm_gain, w_gate, w_up, w_down, expert_ids, gate_logits):
    rows, width = tokens.shape[1:]
    lanes = rows // (2 * GROUPS)
    block = (STOPS, GROUPS, 2)
    anywhere = pl.BlockSpec(memory_space=pl.ANY)
    out = pl.pallas_call(
        kernel,
        out_shape=jax.ShapeDtypeStruct((width, rows), jnp.bfloat16),
        in_specs=[anywhere] * 7,
        out_specs=anywhere,
        scratch_shapes=[
            pltpu.VMEM(block + (SIDE, SIDE, width, lanes), jnp.bfloat16),
            pltpu.VMEM(block + (SIDE, SIDE, width, lanes), jnp.bfloat16),
            pltpu.VMEM(block + (3, SIDE, width, lanes), jnp.bfloat16),
            pltpu.VMEM(block + (SIDE + 1, width, lanes), jnp.bfloat16),
            pltpu.VMEM(block + (SIDE + 3, width, lanes), jnp.bfloat16),
            pltpu.VMEM(block + (width, lanes), jnp.bfloat16),
            pltpu.VMEM((GROUPS, 2, width, lanes), jnp.bfloat16),
            pltpu.VMEM((width, 128), jnp.bfloat16),
            pltpu.VMEM((SIDE, SIDE, width, 128), jnp.bfloat16),
            pltpu.VMEM((STOPS, GROUPS, 1, 2 * lanes), jnp.float32),
            pltpu.VMEM((D, D), jnp.bfloat16),
            pltpu.VMEM((D, D), jnp.bfloat16),
            pltpu.VMEM((D, D), jnp.bfloat16),
            pltpu.VMEM((3, D, D), jnp.bfloat16),
            pltpu.VMEM((1, width), jnp.bfloat16),
            pltpu.VMEM((STOPS, 2, rows), jnp.int32),
            pltpu.VMEM((STOPS, 2, rows), jnp.float32),
            pltpu.SemaphoreType.DMA((4, STOPS, GROUPS)),
            pltpu.SemaphoreType.DMA((4,)),
            pltpu.SemaphoreType.DMA((2,)),
            pltpu.SemaphoreType.DMA((2,)),
            pltpu.SemaphoreType.DMA((6,)),
            pltpu.SemaphoreType.DMA((GROUPS, 2)),
        ],
        compiler_params=pltpu.CompilerParams(
            collective_id=0, has_side_effects=True, vmem_limit_bytes=56 << 20
        ),
    )(
        tokens[0].T, norm_gain, expert_ids[0].transpose(0, 2, 1), gate_logits[0].transpose(0, 2, 1),
        w_gate[0], w_up[0], w_down[0],
    )
    return out.T[None]


def solution(mesh):
    placed = (
        P("section", "dp", "expert"),
        P("section", "expert"),
        P("section", None, "expert"),
        P("section", None, "expert"),
        P("section", "expert", None),
        P("section", None, "dp", None),
        P("section", None, "dp", None),
    )
    return jax.shard_map(
        per_device,
        mesh=mesh,
        in_specs=placed,
        out_specs=P("section", "dp", "expert"),
        check_vma=False,
    )
```

```python
import jax
import jax.numpy as jnp
from jax import lax
from jax.experimental import pallas as pl
from jax.experimental.pallas import tpu as pltpu
from jax.sharding import PartitionSpec as P

D = 768
STOPS = 4
GROUPS = 4
SIDE = 4
SLICE = 48
PIECE = 256
MESH = pl.DeviceIdType.MESH


def kernel(
    tokens_ref, gain_in, ids_in, logits_in, gate_ref, up_ref, down_ref,
    out_ref,
    gathered, partial, returned, summed, last, held, final, gain_own, gain_all, weight,
    gate_t, up_t, down_t, raw, gain_ref, ids_ref, logits_ref,
    recv_sem, send_sem, gain_recv, gain_send, load_sem, out_sem,
):
    section = lax.axis_index("section")
    chip = lax.axis_index("expert")
    plane = lax.axis_index("dp")
    y, x = chip // SIDE, lax.rem(chip, SIDE)
    lanes = gathered.shape[-1]

    def device(core, row, column):
        return (core, row * SIDE + column, plane)

    other = 1 - section
    y_peers = [lax.rem(y + step, SIDE) for step in range(1, SIDE)]
    x_peers = [lax.rem(x + step, SIDE) for step in range(1, SIDE)]

    barrier = pltpu.get_barrier_semaphore()
    partners = [device(other, y, x)]
    for core in (section, other):
        partners += [device(core, row, x) for row in y_peers]
        partners += [device(core, y, column) for column in x_peers]
    for partner in partners:
        pl.semaphore_signal(barrier, inc=1, device_id=partner, device_id_type=MESH)
    loads = [
        pltpu.make_async_copy(source, target, load_sem.at[i])
        for i, (source, target) in enumerate((
            (gain_in, gain_ref), (ids_in, ids_ref), (logits_in, logits_ref),
            (gate_ref, raw.at[0]), (up_ref, raw.at[1]), (down_ref, raw.at[2]),
        ))
    ]
    for load in loads:
        load.start()
    loads[0].wait()
    gain_row = jnp.broadcast_to(gain_ref[...].astype(jnp.float32), (128, SLICE))
    gain_own[...] = gain_row.T.astype(jnp.bfloat16)
    pl.semaphore_wait(barrier, len(partners))

    def send(source, target, send_at, recv_at, to):
        pltpu.make_async_remote_copy(
            src_ref=source, dst_ref=target, send_sem=send_at, recv_sem=recv_at,
            device_id=to, device_id_type=MESH,
        ).start()

    def wait_blocks(sem, blocks):
        view = gathered.at[0, 0].reshape(2 * SIDE * SIDE, SLICE, lanes).at[pl.ds(0, blocks)]
        pltpu.make_async_copy(view, view, sem).wait()

    def wait_gain(sem, blocks):
        view = gain_all.reshape(SIDE * SIDE, SLICE, 128).at[pl.ds(0, blocks)]
        pltpu.make_async_copy(view, view, sem).wait()

    def chip_at(half, on_line, across):
        return (across, on_line) if half == 0 else (on_line, across)

    mine = [(x, y), (y, x)]
    line_peers = [[peers[1], peers[0], peers[2]] for peers in (x_peers, y_peers)]
    before = [lax.rem(place[1] + SIDE - 1, SIDE) for place in mine]
    after = [lax.rem(place[1] + 1, SIDE) for place in mine]
    opposite = [lax.rem(place[1] + 2, SIDE) for place in mine]

    def line(ref, half, across):
        return ref.at[across] if half == 0 else ref.at[:, across]

    def spot(ref, half, on_line, across):
        row, column = chip_at(half, on_line, across)
        return ref.at[row, column]

    def to_chip(core, half, on_line, across):
        return device(core, *chip_at(half, on_line, across))

    def first_step(source, t, g, half, core):
        target = gathered.at[t, g, half, y, x]
        to_recv, to_send = recv_sem.at[0, t, g], send_sem.at[0]
        on_line, across = mine[half]
        send(source, target, to_send, to_recv, to_chip(core, half, on_line, opposite[half]))
        for peer in line_peers[half]:
            send(source, target, to_send, to_recv, to_chip(core, half, peer, across))
        for side in (before, after):
            send(source, target, to_send, to_recv, to_chip(core, half, on_line, side[half]))

    for group in range(GROUPS):
        for half in range(2):
            block = tokens_ref.at[:, pl.ds((2 * group + half) * lanes, lanes)]
            pltpu.make_async_copy(block, gathered.at[0, group, half, y, x], recv_sem.at[0, 0, group]).start()
            first_step(block, 0, group, half, section)
        if group == 0:
            pltpu.make_async_copy(gain_own, gain_all.at[y, x], gain_recv.at[0]).start()
            for peer in y_peers:
                send(gain_own, gain_all.at[y, x], gain_send.at[0], gain_recv.at[0], device(section, peer, x))

    expert = chip // 2
    loads[1].wait()
    loads[2].wait()
    for t in range(STOPS):
        for g in range(GROUPS):
            span = pl.ds(2 * g * lanes, 2 * lanes)
            ids, logits = ids_ref[t, :, span], logits_ref[t, :, span]
            one = jax.nn.sigmoid(logits[0:1] - logits[1:2])
            two = jax.nn.sigmoid(logits[1:2] - logits[0:1])
            weight[t, g] = jnp.where(ids[0:1] == expert, one, 0.0) + jnp.where(ids[1:2] == expert, two, 0.0)

    def spread(t, g):
        wait_blocks(recv_sem.at[0, t, g], 14)
        to_recv, to_send = recv_sem.at[1, t, g], send_sem.at[1]
        for half in range(2):
            on_line, across = mine[half]
            far = spot(gathered.at[t, g, half], half, on_line, opposite[half])
            for peer in line_peers[half]:
                send(far, far, to_send, to_recv, to_chip(section, half, peer, across))
        for side in (before, after):
            for half in range(2):
                on_line, across = mine[half]
                for peer in line_peers[half]:
                    block = spot(gathered.at[t, g, half], half, peer, across)
                    send(block, block, to_send, to_recv, to_chip(section, half, on_line, side[half]))

    def compute(t, g):
        wait_blocks(recv_sem.at[1, t, g], 18)
        acts = jnp.concatenate([gathered[t, g, half].reshape(D, lanes) for half in range(2)], axis=1)
        gain = gain_all[...].reshape(D, 128)
        gain = jnp.concatenate([gain] * (2 * lanes // 128), axis=1)
        acts = acts.astype(jnp.float32)
        scaled = (acts * gain.astype(jnp.float32)).astype(jnp.bfloat16)
        inverse = lax.rsqrt(jnp.sum(acts * acts, axis=0, keepdims=True) / D + 1e-05)
        pieces = []
        for start in range(0, D, PIECE):
            gate_val = jnp.dot(gate_t[start:start + PIECE], scaled, preferred_element_type=jnp.float32) * inverse
            up_val = jnp.dot(up_t[start:start + PIECE], scaled, preferred_element_type=jnp.float32) * inverse
            pieces.append((jax.nn.silu(gate_val) * up_val).astype(jnp.bfloat16))
        hidden = jnp.concatenate(pieces, axis=0)
        outcome = jnp.dot(down_t[...], hidden, preferred_element_type=jnp.float32)
        outcome = (outcome * weight[t, g]).astype(jnp.bfloat16)
        for half in range(2):
            partial[t, g, half] = outcome[:, half * lanes:(half + 1) * lanes].reshape(SIDE, SIDE, SLICE, lanes)
        to_recv, to_send = recv_sem.at[2, t, g], send_sem.at[2]
        for half in range(2):
            on_line, across = mine[half]
            for peer in line_peers[half]:
                send(spot(partial.at[t, g, half], half, peer, opposite[half]), returned.at[t, g, half, 2, on_line],
                     to_send, to_recv, to_chip(section, half, peer, across))
        for side, slot in ((before, 1), (after, 0)):
            for half in range(2):
                on_line, across = mine[half]
                for peer in line_peers[half]:
                    send(spot(partial.at[t, g, half], half, peer, side[half]), returned.at[t, g, half, slot, peer],
                         to_send, to_recv, to_chip(section, half, on_line, side[half]))

    def collect(t, g):
        wait_blocks(recv_sem.at[2, t, g], 18)
        core = lax.rem(section + t // (STOPS - 1), 2)
        to_recv, to_send = recv_sem.at[3, t, g], send_sem.at[3]
        for half in range(2):
            on_line, across = mine[half]
            total = spot(partial.at[t, g, half], half, on_line, opposite[half])[...].astype(jnp.float32)
            for peer in line_peers[half]:
                total = total + returned[t, g, half, 2, peer].astype(jnp.float32)
            summed[t, g, half, SIDE] = total.astype(jnp.bfloat16)
            send(summed.at[t, g, half, SIDE], last.at[t, g, half, SIDE], to_send, to_recv,
                 to_chip(core, half, on_line, opposite[half]))
            for peer in line_peers[half]:
                total = spot(partial.at[t, g, half], half, peer, across)[...].astype(jnp.float32)
                for slot in range(2):
                    total = total + returned[t, g, half, slot, peer].astype(jnp.float32)
                summed[t, g, half, peer] = total.astype(jnp.bfloat16)
                send(summed.at[t, g, half, peer], last.at[t, g, half, on_line], to_send, to_recv,
                     to_chip(core, half, peer, across))
            for side, slot in ((before, SIDE + 2), (after, SIDE + 1)):
                send(spot(partial.at[t, g, half], half, on_line, side[half]), last.at[t, g, half, slot], to_send, to_recv,
                     to_chip(core, half, on_line, side[half]))

            @pl.when(t == STOPS - 1)
            def _(half=half, on_line=on_line):
                send(partial.at[t, g, half, y, x], last.at[t, g, half, on_line], to_send, to_recv, device(other, y, x))
                send(gathered.at[t, g, half, y, x], final.at[g, half], to_send, to_recv, device(other, y, x))

    def finish(t, g):
        @pl.when(t < STOPS - 1)
        def _():
            wait_blocks(recv_sem.at[3, t, g], 12)
            later = jnp.minimum(t + 1, STOPS - 1)
            for half in range(2):
                on_line, across = mine[half]
                total = partial[t, g, half, y, x].astype(jnp.float32)
                for peer in line_peers[half] + [SIDE, SIDE + 1, SIDE + 2]:
                    total = total + last[t, g, half, peer].astype(jnp.float32)
                total = gathered[t, g, half, y, x].astype(jnp.float32) + total
                held[t, g, half] = total.astype(jnp.bfloat16)
                block = held.at[t, g, half]
                first_step(block, later, g, half, other)
                send(block, gathered.at[later, g, half, y, x], send_sem.at[0], recv_sem.at[0, later, g],
                     device(other, y, x))

        @pl.when(t == STOPS - 1)
        def _():
            wait_blocks(recv_sem.at[3, t, g], 16)
            for half in range(2):
                total = jnp.sum(last[t, g, half].astype(jnp.float32), axis=0)
                total = final[g, half].astype(jnp.float32) + total
                held[t, g, half] = total.astype(jnp.bfloat16)
                to_out(t, g, half).start()

    def to_out(t, g, half):
        span = pl.ds(pl.multiple_of((2 * g + half) * lanes, lanes), lanes)
        return pltpu.make_async_copy(held.at[t, g, half], out_ref.at[:, span], out_sem.at[g, half])

    def each_group(stage, t):
        def one(g, carry):
            stage(t, g)
            return carry
        lax.fori_loop(0, GROUPS, one, 0)

    for g in range(GROUPS):
        spread(0, g)
        if g == 0:
            wait_gain(gain_recv.at[0], 4)
            for peer in x_peers:
                send(gain_all.at[:, x], gain_all.at[:, x], gain_send.at[1], gain_recv.at[1], device(section, y, peer))
    for i, target in enumerate((gate_t, up_t, down_t)):
        loads[i + 3].wait()
        target[...] = raw[i].T
    wait_gain(gain_recv.at[1], 12)

    def stop(t, carry):
        each_group(compute, t)
        for g in range(GROUPS):
            collect(t, g)
        for g in range(GROUPS):
            finish(t, g)

        @pl.when(t < STOPS - 1)
        def _():
            for g in range(GROUPS):
                spread(jnp.minimum(t + 1, STOPS - 1), g)
        return carry

    lax.fori_loop(0, STOPS, stop, 0)

    steps = STOPS * GROUPS
    sent = (12 * GROUPS + 14 * (steps - GROUPS), 18 * steps, 18 * steps, 12 * (steps - GROUPS) + 16 * GROUPS)
    for k, blocks in enumerate(sent):
        view = gathered.reshape(steps * 2 * SIDE * SIDE, SLICE, lanes).at[pl.ds(0, blocks)]
        pltpu.make_async_copy(view, view, send_sem.at[k]).wait()
    wait_gain(gain_send.at[0], 3)
    wait_gain(gain_send.at[1], 12)
    for g in range(GROUPS):
        for half in range(2):
            to_out(STOPS - 1, g, half).wait()


def per_device(tokens, norm_gain, w_gate, w_up, w_down, expert_ids, gate_logits):
    rows, width = tokens.shape[1:]
    lanes = rows // (2 * GROUPS)
    block = (STOPS, GROUPS, 2)
    anywhere = pl.BlockSpec(memory_space=pl.ANY)
    out = pl.pallas_call(
        kernel,
        out_shape=jax.ShapeDtypeStruct((width, rows), jnp.bfloat16),
        in_specs=[anywhere] * 7,
        out_specs=anywhere,
        scratch_shapes=[
            pltpu.VMEM(block + (SIDE, SIDE, width, lanes), jnp.bfloat16),
            pltpu.VMEM(block + (SIDE, SIDE, width, lanes), jnp.bfloat16),
            pltpu.VMEM(block + (3, SIDE, width, lanes), jnp.bfloat16),
            pltpu.VMEM(block + (SIDE + 1, width, lanes), jnp.bfloat16),
            pltpu.VMEM(block + (SIDE + 3, width, lanes), jnp.bfloat16),
            pltpu.VMEM(block + (width, lanes), jnp.bfloat16),
            pltpu.VMEM((GROUPS, 2, width, lanes), jnp.bfloat16),
            pltpu.VMEM((width, 128), jnp.bfloat16),
            pltpu.VMEM((SIDE, SIDE, width, 128), jnp.bfloat16),
            pltpu.VMEM((STOPS, GROUPS, 1, 2 * lanes), jnp.float32),
            pltpu.VMEM((D, D), jnp.bfloat16),
            pltpu.VMEM((D, D), jnp.bfloat16),
            pltpu.VMEM((D, D), jnp.bfloat16),
            pltpu.VMEM((3, D, D), jnp.bfloat16),
            pltpu.VMEM((1, width), jnp.bfloat16),
            pltpu.VMEM((STOPS, 2, rows), jnp.int32),
            pltpu.VMEM((STOPS, 2, rows), jnp.float32),
            pltpu.SemaphoreType.DMA((4, STOPS, GROUPS)),
            pltpu.SemaphoreType.DMA((4,)),
            pltpu.SemaphoreType.DMA((2,)),
            pltpu.SemaphoreType.DMA((2,)),
            pltpu.SemaphoreType.DMA((6,)),
            pltpu.SemaphoreType.DMA((GROUPS, 2)),
        ],
        compiler_params=pltpu.CompilerParams(
            collective_id=0, has_side_effects=True, vmem_limit_bytes=56 << 20
        ),
    )(
        tokens[0].T, norm_gain, expert_ids[0].transpose(0, 2, 1), gate_logits[0].transpose(0, 2, 1),
        w_gate[0], w_up[0], w_down[0],
    )
    return out.T[None]


def solution(mesh):
    placed = (
        P("section", "dp", "expert"),
        P("section", "expert"),
        P("section", None, "expert"),
        P("section", None, "expert"),
        P("section", "expert", None),
        P("section", None, "dp", None),
        P("section", None, "dp", None),
    )
    return jax.shard_map(
        per_device,
        mesh=mesh,
        in_specs=placed,
        out_specs=P("section", "dp", "expert"),
        check_vma=False,
    )
```

```python
import jax
import jax.numpy as jnp
from jax import lax
from jax.experimental import pallas as pl
from jax.experimental.pallas import tpu as pltpu
from jax.sharding import PartitionSpec as P

D = 768
STOPS = 4
GROUPS = 4
SIDE = 4
SLICE = 48
PIECE = 256
MESH = pl.DeviceIdType.MESH


def kernel(
    tokens_in, gain_in, ids_in, logits_in, gate_ref, up_ref, down_ref,
    out_ref,
    gathered, partial, returned, summed, last, held, final, gain_own, gain_all, weight,
    gate_t, up_t, down_t, raw, gain_ref, ids_ref, logits_ref, tokens_ref,
    recv_sem, send_sem, gain_recv, gain_send, load_sem, out_sem,
):
    section = lax.axis_index("section")
    chip = lax.axis_index("expert")
    plane = lax.axis_index("dp")
    y, x = chip // SIDE, lax.rem(chip, SIDE)
    lanes = gathered.shape[-1]

    def device(core, row, column):
        return (core, row * SIDE + column, plane)

    other = 1 - section
    y_peers = [lax.rem(y + step, SIDE) for step in range(1, SIDE)]
    x_peers = [lax.rem(x + step, SIDE) for step in range(1, SIDE)]

    barrier = pltpu.get_barrier_semaphore()
    partners = [device(other, y, x)]
    for core in (section, other):
        partners += [device(core, row, x) for row in y_peers]
        partners += [device(core, y, column) for column in x_peers]
    for partner in partners:
        pl.semaphore_signal(barrier, inc=1, device_id=partner, device_id_type=MESH)
    loads = [
        pltpu.make_async_copy(source, target, load_sem.at[i])
        for i, (source, target) in enumerate((
            (gain_in, gain_ref), (ids_in, ids_ref), (logits_in, logits_ref),
            (gate_ref, raw.at[0]), (up_ref, raw.at[1]), (down_ref, raw.at[2]), (tokens_in, tokens_ref),
        ))
    ]
    for load in loads[6:] + loads[:3]:
        load.start()
    loads[0].wait()
    gain_row = jnp.broadcast_to(gain_ref[...].astype(jnp.float32), (128, SLICE))
    gain_own[...] = gain_row.T.astype(jnp.bfloat16)
    loads[6].wait()
    pl.semaphore_wait(barrier, len(partners))

    def send(source, target, send_at, recv_at, to):
        pltpu.make_async_remote_copy(
            src_ref=source, dst_ref=target, send_sem=send_at, recv_sem=recv_at,
            device_id=to, device_id_type=MESH,
        ).start()

    def wait_blocks(sem, blocks):
        view = gathered.at[0, 0].reshape(2 * SIDE * SIDE, SLICE, lanes).at[pl.ds(0, blocks)]
        pltpu.make_async_copy(view, view, sem).wait()

    def wait_gain(sem, blocks):
        view = gain_all.reshape(SIDE * SIDE, SLICE, 128).at[pl.ds(0, blocks)]
        pltpu.make_async_copy(view, view, sem).wait()

    def chip_at(half, on_line, across):
        return (across, on_line) if half == 0 else (on_line, across)

    mine = [(x, y), (y, x)]
    line_peers = [[peers[1], peers[0], peers[2]] for peers in (x_peers, y_peers)]
    before = [lax.rem(place[1] + SIDE - 1, SIDE) for place in mine]
    after = [lax.rem(place[1] + 1, SIDE) for place in mine]
    opposite = [lax.rem(place[1] + 2, SIDE) for place in mine]

    def line(ref, half, across):
        return ref.at[across] if half == 0 else ref.at[:, across]

    def spot(ref, half, on_line, across):
        row, column = chip_at(half, on_line, across)
        return ref.at[row, column]

    def to_chip(core, half, on_line, across):
        return device(core, *chip_at(half, on_line, across))

    def first_step(source, t, g, half, core):
        target = gathered.at[t, g, half, y, x]
        to_recv, to_send = recv_sem.at[0, t, g], send_sem.at[0]
        on_line, across = mine[half]
        send(source, target, to_send, to_recv, to_chip(core, half, on_line, opposite[half]))
        for peer in line_peers[half]:
            send(source, target, to_send, to_recv, to_chip(core, half, peer, across))
        for side in (before, after):
            send(source, target, to_send, to_recv, to_chip(core, half, on_line, side[half]))

    for group in range(GROUPS):
        for half in range(2):
            block = tokens_ref.at[:, pl.ds((2 * group + half) * lanes, lanes)]
            pltpu.make_async_copy(block, gathered.at[0, group, half, y, x], recv_sem.at[0, 0, group]).start()
            first_step(block, 0, group, half, section)
        if group == 0:
            pltpu.make_async_copy(gain_own, gain_all.at[y, x], gain_recv.at[0]).start()
            for peer in y_peers:
                send(gain_own, gain_all.at[y, x], gain_send.at[0], gain_recv.at[0], device(section, peer, x))

    for load in loads[3:6]:
        load.start()

    expert = chip // 2
    loads[1].wait()
    loads[2].wait()
    for t in range(STOPS):
        for g in range(GROUPS):
            span = pl.ds(2 * g * lanes, 2 * lanes)
            ids, logits = ids_ref[t, :, span], logits_ref[t, :, span]
            one = jax.nn.sigmoid(logits[0:1] - logits[1:2])
            two = jax.nn.sigmoid(logits[1:2] - logits[0:1])
            weight[t, g] = jnp.where(ids[0:1] == expert, one, 0.0) + jnp.where(ids[1:2] == expert, two, 0.0)

    def spread(t, g):
        wait_blocks(recv_sem.at[0, t, g], 14)
        to_recv, to_send = recv_sem.at[1, t, g], send_sem.at[1]
        for half in range(2):
            on_line, across = mine[half]
            far = spot(gathered.at[t, g, half], half, on_line, opposite[half])
            for peer in line_peers[half]:
                send(far, far, to_send, to_recv, to_chip(section, half, peer, across))
        for side in (before, after):
            for half in range(2):
                on_line, across = mine[half]
                for peer in line_peers[half]:
                    block = spot(gathered.at[t, g, half], half, peer, across)
                    send(block, block, to_send, to_recv, to_chip(section, half, on_line, side[half]))

    def compute(t, g):
        wait_blocks(recv_sem.at[1, t, g], 18)
        acts = jnp.concatenate([gathered[t, g, half].reshape(D, lanes) for half in range(2)], axis=1)
        gain = gain_all[...].reshape(D, 128)
        gain = jnp.concatenate([gain] * (2 * lanes // 128), axis=1)
        acts = acts.astype(jnp.float32)
        scaled = (acts * gain.astype(jnp.float32)).astype(jnp.bfloat16)
        inverse = lax.rsqrt(jnp.sum(acts * acts, axis=0, keepdims=True) / D + 1e-05)
        pieces = []
        for start in range(0, D, PIECE):
            gate_val = jnp.dot(gate_t[start:start + PIECE], scaled, preferred_element_type=jnp.float32) * inverse
            up_val = jnp.dot(up_t[start:start + PIECE], scaled, preferred_element_type=jnp.float32) * inverse
            pieces.append((jax.nn.silu(gate_val) * up_val).astype(jnp.bfloat16))
        hidden = jnp.concatenate(pieces, axis=0)
        outcome = jnp.dot(down_t[...], hidden, preferred_element_type=jnp.float32)
        outcome = (outcome * weight[t, g]).astype(jnp.bfloat16)
        for half in range(2):
            partial[t, g, half] = outcome[:, half * lanes:(half + 1) * lanes].reshape(SIDE, SIDE, SLICE, lanes)
        to_recv, to_send = recv_sem.at[2, t, g], send_sem.at[2]
        for half in range(2):
            on_line, across = mine[half]
            for peer in line_peers[half]:
                send(spot(partial.at[t, g, half], half, peer, opposite[half]), returned.at[t, g, half, 2, on_line],
                     to_send, to_recv, to_chip(section, half, peer, across))
        for side, slot in ((before, 1), (after, 0)):
            for half in range(2):
                on_line, across = mine[half]
                for peer in line_peers[half]:
                    send(spot(partial.at[t, g, half], half, peer, side[half]), returned.at[t, g, half, slot, peer],
                         to_send, to_recv, to_chip(section, half, on_line, side[half]))

    def collect(t, g):
        wait_blocks(recv_sem.at[2, t, g], 18)
        core = lax.rem(section + t // (STOPS - 1), 2)
        to_recv, to_send = recv_sem.at[3, t, g], send_sem.at[3]
        for half in range(2):
            on_line, across = mine[half]
            total = spot(partial.at[t, g, half], half, on_line, opposite[half])[...].astype(jnp.float32)
            for peer in line_peers[half]:
                total = total + returned[t, g, half, 2, peer].astype(jnp.float32)
            summed[t, g, half, SIDE] = total.astype(jnp.bfloat16)
            send(summed.at[t, g, half, SIDE], last.at[t, g, half, SIDE], to_send, to_recv,
                 to_chip(core, half, on_line, opposite[half]))
            for peer in line_peers[half]:
                total = spot(partial.at[t, g, half], half, peer, across)[...].astype(jnp.float32)
                for slot in range(2):
                    total = total + returned[t, g, half, slot, peer].astype(jnp.float32)
                summed[t, g, half, peer] = total.astype(jnp.bfloat16)
                send(summed.at[t, g, half, peer], last.at[t, g, half, on_line], to_send, to_recv,
                     to_chip(core, half, peer, across))
            for side, slot in ((before, SIDE + 2), (after, SIDE + 1)):
                send(spot(partial.at[t, g, half], half, on_line, side[half]), last.at[t, g, half, slot], to_send, to_recv,
                     to_chip(core, half, on_line, side[half]))

            @pl.when(t == STOPS - 1)
            def _(half=half, on_line=on_line):
                send(partial.at[t, g, half, y, x], last.at[t, g, half, on_line], to_send, to_recv, device(other, y, x))
                send(gathered.at[t, g, half, y, x], final.at[g, half], to_send, to_recv, device(other, y, x))

    def finish(t, g):
        @pl.when(t < STOPS - 1)
        def _():
            wait_blocks(recv_sem.at[3, t, g], 12)
            later = jnp.minimum(t + 1, STOPS - 1)
            for half in range(2):
                on_line, across = mine[half]
                total = partial[t, g, half, y, x].astype(jnp.float32)
                for peer in line_peers[half] + [SIDE, SIDE + 1, SIDE + 2]:
                    total = total + last[t, g, half, peer].astype(jnp.float32)
                total = gathered[t, g, half, y, x].astype(jnp.float32) + total
                held[t, g, half] = total.astype(jnp.bfloat16)
                block = held.at[t, g, half]
                first_step(block, later, g, half, other)
                send(block, gathered.at[later, g, half, y, x], send_sem.at[0], recv_sem.at[0, later, g],
                     device(other, y, x))

        @pl.when(t == STOPS - 1)
        def _():
            wait_blocks(recv_sem.at[3, t, g], 16)
            for half in range(2):
                total = jnp.sum(last[t, g, half].astype(jnp.float32), axis=0)
                total = final[g, half].astype(jnp.float32) + total
                held[t, g, half] = total.astype(jnp.bfloat16)
                to_out(t, g, half).start()

    def to_out(t, g, half):
        span = pl.ds(pl.multiple_of((2 * g + half) * lanes, lanes), lanes)
        return pltpu.make_async_copy(held.at[t, g, half], out_ref.at[:, span], out_sem.at[g, half])

    def each_group(stage, t):
        def one(g, carry):
            stage(t, g)
            return carry
        lax.fori_loop(0, GROUPS, one, 0)

    for g in range(GROUPS):
        spread(0, g)
        if g == 0:
            wait_gain(gain_recv.at[0], 4)
            for peer in x_peers:
                send(gain_all.at[:, x], gain_all.at[:, x], gain_send.at[1], gain_recv.at[1], device(section, y, peer))
    for i, target in enumerate((gate_t, up_t, down_t)):
        loads[i + 3].wait()
        target[...] = raw[i].T
    wait_gain(gain_recv.at[1], 12)

    def stop(t, carry):
        each_group(compute, t)
        for g in range(GROUPS):
            collect(t, g)
        for g in range(GROUPS):
            finish(t, g)

        @pl.when(t < STOPS - 1)
        def _():
            for g in range(GROUPS):
                spread(jnp.minimum(t + 1, STOPS - 1), g)
        return carry

    lax.fori_loop(0, STOPS, stop, 0)

    steps = STOPS * GROUPS
    sent = (12 * GROUPS + 14 * (steps - GROUPS), 18 * steps, 18 * steps, 12 * (steps - GROUPS) + 16 * GROUPS)
    for k, blocks in enumerate(sent):
        view = gathered.reshape(steps * 2 * SIDE * SIDE, SLICE, lanes).at[pl.ds(0, blocks)]
        pltpu.make_async_copy(view, view, send_sem.at[k]).wait()
    wait_gain(gain_send.at[0], 3)
    wait_gain(gain_send.at[1], 12)
    for g in range(GROUPS):
        for half in range(2):
            to_out(STOPS - 1, g, half).wait()


def per_device(tokens, norm_gain, w_gate, w_up, w_down, expert_ids, gate_logits):
    rows, width = tokens.shape[1:]
    lanes = rows // (2 * GROUPS)
    block = (STOPS, GROUPS, 2)
    anywhere = pl.BlockSpec(memory_space=pl.ANY)
    out = pl.pallas_call(
        kernel,
        out_shape=jax.ShapeDtypeStruct((width, rows), jnp.bfloat16),
        in_specs=[anywhere] * 7,
        out_specs=anywhere,
        scratch_shapes=[
            pltpu.VMEM(block + (SIDE, SIDE, width, lanes), jnp.bfloat16),
            pltpu.VMEM(block + (SIDE, SIDE, width, lanes), jnp.bfloat16),
            pltpu.VMEM(block + (3, SIDE, width, lanes), jnp.bfloat16),
            pltpu.VMEM(block + (SIDE + 1, width, lanes), jnp.bfloat16),
            pltpu.VMEM(block + (SIDE + 3, width, lanes), jnp.bfloat16),
            pltpu.VMEM(block + (width, lanes), jnp.bfloat16),
            pltpu.VMEM((GROUPS, 2, width, lanes), jnp.bfloat16),
            pltpu.VMEM((width, 128), jnp.bfloat16),
            pltpu.VMEM((SIDE, SIDE, width, 128), jnp.bfloat16),
            pltpu.VMEM((STOPS, GROUPS, 1, 2 * lanes), jnp.float32),
            pltpu.VMEM((D, D), jnp.bfloat16),
            pltpu.VMEM((D, D), jnp.bfloat16),
            pltpu.VMEM((D, D), jnp.bfloat16),
            pltpu.VMEM((3, D, D), jnp.bfloat16),
            pltpu.VMEM((1, width), jnp.bfloat16),
            pltpu.VMEM((STOPS, 2, rows), jnp.int32),
            pltpu.VMEM((STOPS, 2, rows), jnp.float32),
            pltpu.VMEM((width, rows), jnp.bfloat16),
            pltpu.SemaphoreType.DMA((4, STOPS, GROUPS)),
            pltpu.SemaphoreType.DMA((4,)),
            pltpu.SemaphoreType.DMA((2,)),
            pltpu.SemaphoreType.DMA((2,)),
            pltpu.SemaphoreType.DMA((7,)),
            pltpu.SemaphoreType.DMA((GROUPS, 2)),
        ],
        compiler_params=pltpu.CompilerParams(
            collective_id=0, has_side_effects=True, vmem_limit_bytes=56 << 20
        ),
    )(
        tokens[0].T, norm_gain, expert_ids[0].transpose(0, 2, 1), gate_logits[0].transpose(0, 2, 1),
        w_gate[0], w_up[0], w_down[0],
    )
    return out.T[None]


def solution(mesh):
    placed = (
        P("section", "dp", "expert"),
        P("section", "expert"),
        P("section", None, "expert"),
        P("section", None, "expert"),
        P("section", "expert", None),
        P("section", None, "dp", None),
        P("section", None, "dp", None),
    )
    return jax.shard_map(
        per_device,
        mesh=mesh,
        in_specs=placed,
        out_specs=P("section", "dp", "expert"),
        check_vma=False,
    )
```
